32 devices in a mesh: rep: 8 (over z, x), shard: 4 (over y, core).
Axes of the slice: x: 2, y: 2, z: 4, core: 2. Of those that a mesh axis runs over, the one named last changes fastest.
Arguments:
- tokens: bfloat16 [49152, 960], P(('rep', 'shard')), may hold values from -6 to 6
- lengths: int32 [32], P(('rep', 'shard')), may hold values from 1024 to 1536, as said below
- cotangent: bfloat16 [49152, 960], P(('rep', 'shard')), may hold values from -6 to 6
- w_query: bfloat16 [960, 960], P('shard'), may hold values from -0.1875 to 0.1875
- w_key: bfloat16 [960, 320], P('shard'), may hold values from -0.1875 to 0.1875
- w_value: bfloat16 [960, 320], P('shard'), may hold values from -0.1875 to 0.1875
- w_out: bfloat16 [960, 960], P('shard'), may hold values from -0.5 to 0.5
- w_gate: bfloat16 [960, 2560], P('shard'), may hold values from -0.1875 to 0.1875
- w_up: bfloat16 [960, 2560], P('shard'), may hold values from -0.1875 to 0.1875
- w_down: bfloat16 [2560, 960], P('shard'), may hold values from -0.125 to 0.125
- gain_attn: bfloat16 [960], P('shard'), may hold values from 0.5 to 1.5
- gain_ffn: bfloat16 [960], P('shard'), may hold values from 0.5 to 1.5
Outputs:
- output: float32 [49152, 960], P(('rep', 'shard'))
- grad_tokens: float32 [49152, 960], P(('rep', 'shard'))
- grad_query: float32 [960, 960], P('shard')
- grad_key: float32 [960, 320], P('shard')
- grad_value: float32 [960, 320], P('shard')
- grad_outproj: float32 [960, 960], P('shard')
- grad_gate: float32 [960, 2560], P('shard')
- grad_up: float32 [960, 2560], P('shard')
- grad_down: float32 [2560, 960], P('shard')
- grad_gain_attn: float32 [960], P('shard')
- grad_gain_ffn: float32 [960], P('shard')
The draws below stay inside these ranges and needn't reach their ends.
Inputs may be any that keep to these rules, and one draw needn't show every extreme that they name: `lengths`: some block holds a sequence of 1536 tokens and some one of 1024.
All inputs are finite; a program needn't handle non-finite values.
Results may differ from the reference program's by a relative error of at most 0.017.
Values may be sent and summed in bfloat16 or wider, within the bound.
A program may use at most 320 MiB of HBM per device.

```python
import jax
import jax.numpy as jnp
from jax import lax

D = 960
HEADS = 15
KV_HEADS = 5
HEAD_DIM = 64
FF = 2560
CAP = 1536
MIN_LEN = 1024
QBLK = 512
ROWS = 49152
DEVICES = 32


def draw_lengths(key, part):
    key = jax.random.fold_in(key, 11)
    key_lengths, key_long, key_short = jax.random.split(key, 3)
    lengths = jax.random.randint(key_lengths, (DEVICES,), MIN_LEN, CAP + 1)
    longest = jax.random.randint(key_long, (), 0, DEVICES)
    shortest = (longest + 1 + jax.random.randint(key_short, (), 0, DEVICES - 1)) % DEVICES
    return lengths.at[longest].set(CAP).at[shortest].set(MIN_LEN).astype(jnp.int32)


def block_scale(key, shape, cuts, smallest, high):
    gain = 1.0
    for axis_at, blocks in cuts:
        heights = jax.random.uniform(jax.random.fold_in(jax.random.fold_in(key, 6), axis_at), (blocks,), jnp.float32, smallest / len(cuts), high / len(cuts))
        gain = gain * jnp.repeat(jnp.exp(heights), shape[axis_at] // blocks).reshape((-1,) + (1,) * (len(shape) - 1 - axis_at))
    return gain


def noise(stream_key, extent, scale, most, cuts=(), kind=jnp.bfloat16):
    gain = block_scale(stream_key, extent, cuts, -0.22, 0.18) if cuts else 1.0
    values = jax.random.normal(stream_key, extent, jnp.float32) * scale * gain
    return jnp.minimum(jnp.maximum(values, -most), most).astype(kind)


def setup_inputs(seed: int = 0) -> dict:
    keys = jax.random.split(jax.random.key(seed), 13)
    tokens = noise(keys[0], (ROWS, D), 1.0, 6.0, ((0, 32),))
    lengths = draw_lengths(jax.random.fold_in(keys[12], 71), 0)
    cotangent = noise(keys[2], (ROWS, D), 1.0, 6.0, ((0, 32),))
    w_query = noise(keys[3], (D, D), D ** -0.5, 0.1875, ((0, 4),))
    w_key = noise(keys[4], (D, KV_HEADS * HEAD_DIM), D ** -0.5, 0.1875, ((0, 4),))
    w_value = noise(keys[5], (D, KV_HEADS * HEAD_DIM), D ** -0.5, 0.1875, ((0, 4),))
    w_out = noise(keys[6], (D, D), (D // 8) ** -0.5, 0.5, ((0, 4),))
    w_gate = noise(keys[7], (D, FF), D ** -0.5, 0.1875, ((0, 4),))
    w_up = noise(keys[8], (D, FF), D ** -0.5, 0.1875, ((0, 4),))
    w_down = noise(keys[9], (FF, D), FF ** -0.5, 0.125, ((0, 4),))
    gain_attn = jnp.clip(1.0 + 0.1 * jax.random.normal(keys[10], (D,), jnp.float32), 0.5, 1.5).astype(jnp.bfloat16)
    gain_ffn = jnp.clip(1.0 + 0.1 * jax.random.normal(keys[11], (D,), jnp.float32), 0.5, 1.5).astype(jnp.bfloat16)
    return {"tokens": tokens, "lengths": lengths, "cotangent": cotangent, "w_query": w_query, "w_key": w_key, "w_value": w_value, "w_out": w_out, "w_gate": w_gate, "w_up": w_up, "w_down": w_down, "gain_attn": gain_attn, "gain_ffn": gain_ffn}


EPS = 1e-05
THETA = 10000.0
NEGATIVE = -1e+30

@jax.custom_vjp
def low(v):
    return lax.optimization_barrier(v.astype(jnp.bfloat16)).astype(jnp.float32)

@jax.custom_vjp
def low_back(v):
    return v

def low_keep(v):
    return (low(v), None)

def low_pass(kept, grad):
    return (grad,)

def back_keep(v):
    return (v, None)

def back_low(kept, grad):
    return (low(grad),)
low.defvjp(low_keep, low_pass)
low_back.defvjp(back_keep, back_low)

def product(left, right):
    return jnp.dot(left, right, precision=lax.Precision.HIGHEST)

def tables():
    half = HEAD_DIM // 2
    position = jnp.arange(CAP, dtype=jnp.float32)
    frequency = THETA ** (-jnp.arange(half, dtype=jnp.float32) * 2.0 / HEAD_DIM)
    angle = position[:, None] * frequency[None, :]
    return (jnp.cos(angle)[:, None, :], jnp.sin(angle)[:, None, :])

def rotate(tensor, cosine, sine):
    half = HEAD_DIM // 2
    first_half = tensor[..., :half]
    second_half = tensor[..., half:]
    return jnp.concatenate([first_half * cosine - second_half * sine, second_half * cosine + first_half * sine], -1)

def attend(query_rot, key_rot, value_low):
    group_size = HEADS // KV_HEADS
    factor = HEAD_DIM ** (-0.5)

    def block(block_index):
        first_row = block_index * QBLK
        query_block = lax.dynamic_slice_in_dim(query_rot, first_row, QBLK, 0)
        raw_scores = low_back(jnp.einsum('qgrd,kgd->grqk', query_block, key_rot, precision=lax.Precision.HIGHEST))
        scores = raw_scores * factor
        query_pos = first_row + jnp.arange(QBLK, dtype=jnp.int32)
        key_pos = jnp.arange(CAP, dtype=jnp.int32)
        scores = jnp.where(key_pos[None, :] <= query_pos[:, None], scores, NEGATIVE)
        row_max = lax.optimization_barrier(jnp.max(scores, -1, keepdims=True))
        raised = jnp.exp(scores - row_max)
        attn_prob = raised / lax.optimization_barrier(jnp.sum(raised, -1, keepdims=True))
        return jnp.einsum('grqk,kgd->qgrd', low(attn_prob), value_low, precision=lax.Precision.HIGHEST)
    blocks = lax.map(jax.checkpoint(block), jnp.arange(CAP // QBLK, dtype=jnp.int32))
    return blocks.reshape(CAP, D)

def forward(inputs, live_mask, params):
    w_query, w_key, w_value, w_out, w_gate, w_up, w_down, gain_attn, gain_ffn = params
    group_size = HEADS // KV_HEADS
    cosine, sine = tables()
    scale_one = lax.rsqrt(lax.optimization_barrier(jnp.mean(inputs * inputs, -1, keepdims=True)) + EPS)
    hidden_one = low(inputs * scale_one * gain_attn)
    queries = low_back(product(hidden_one, w_query)).reshape(CAP, HEADS, HEAD_DIM)
    keys_raw = low_back(product(hidden_one, w_key)).reshape(CAP, KV_HEADS, HEAD_DIM)
    values_low = low_back(low(product(hidden_one, w_value))).reshape(CAP, KV_HEADS, HEAD_DIM)
    query_rot = low(rotate(queries, cosine, sine)).reshape(CAP, KV_HEADS, group_size, HEAD_DIM)
    key_rot = low(rotate(keys_raw, cosine, sine))
    attn_low = low_back(low(attend(query_rot, key_rot, values_low)))
    mixed = inputs + low_back(product(attn_low, w_out))
    scale_two = lax.rsqrt(lax.optimization_barrier(jnp.mean(mixed * mixed, -1, keepdims=True)) + EPS)
    hidden_two = low(mixed * scale_two * gain_ffn)
    gate = low_back(product(hidden_two, w_gate))
    up_proj = low_back(product(hidden_two, w_up))
    product_low = low_back(low(jax.nn.silu(gate) * up_proj))
    return (mixed + low_back(product(product_low, w_down))) * live_mask

def reference(tokens, lengths, cotangent, w_query, w_key, w_value, w_out, w_gate, w_up, w_down, gain_attn, gain_ffn):
    params = (w_query.astype(jnp.float32), w_key.astype(jnp.float32), w_value.astype(jnp.float32), w_out.astype(jnp.float32), w_gate.astype(jnp.float32), w_up.astype(jnp.float32), w_down.astype(jnp.float32), gain_attn.astype(jnp.float32), gain_ffn.astype(jnp.float32))
    sequences = tokens.astype(jnp.float32).reshape(DEVICES, CAP, D)
    cotangents = cotangent.astype(jnp.float32).reshape(DEVICES, CAP, D)

    def visit(summed, item):
        inputs, seq_cot, length = item
        live_mask = (jnp.arange(CAP, dtype=jnp.int32) < length).astype(jnp.float32)[:, None]
        result, pullback = jax.vjp(lambda given, weights: forward(given, live_mask, weights), inputs, params)
        grad_inputs, grad_params = pullback(seq_cot)
        summed = jax.tree.map(lambda older, newer: older + newer, summed, grad_params)
        return (summed, (result, grad_inputs))
    zeros = jax.tree.map(jnp.zeros_like, params)
    grads, (results, grad_rows) = lax.scan(visit, zeros, (sequences, cotangents, lengths))
    return (results.reshape(ROWS, D), grad_rows.reshape(ROWS, D), grads[0], grads[1], grads[2], grads[3], grads[4], grads[5], grads[6], grads[7], grads[8])
```

```python
import jax
import jax.numpy as jnp
from jax import lax
from jax.experimental import pallas as pl
from jax.experimental.pallas import tpu as pltpu
from jax.sharding import PartitionSpec as P

D = 960
HEADS = 15
KV_HEADS = 5
HEAD_DIM = 64
GROUP = HEADS // KV_HEADS
KV = KV_HEADS * HEAD_DIM
QB = 256
SCALE = HEAD_DIM ** (-0.5)
EPS = 1e-05
THETA = 10000.0
NEGATIVE = -1e30
VMEM = 48 * 1024 * 1024


def dot(left, right, contract):
    return lax.dot_general(
        left, right, ((contract[:1], contract[1:]), ((), ())), preferred_element_type=jnp.float32
    )


def diagonal(scores):
    keys = lax.broadcasted_iota(jnp.int32, scores.shape, 0)
    queries = lax.broadcasted_iota(jnp.int32, scores.shape, 1)
    return jnp.where(keys <= queries, scores, NEGATIVE)


def forward_kernel(q_ref, k_ref, v_ref, out_ref, log_ref):
    rows = q_ref.shape[1]
    key_rows = k_ref[...].T
    for start in range(0, rows, QB):
        stop = start + QB
        query = q_ref[:, start:stop]
        low = diagonal(dot(key_rows[start:stop], query, (1, 0)))
        top = jnp.max(low, 0, keepdims=True)
        if start:
            high = dot(key_rows[:start], query, (1, 0))
            top = jnp.maximum(top, jnp.max(high, 0, keepdims=True))
        low = jnp.exp(low - top)
        total = jnp.sum(low, 0, keepdims=True)
        mixed = dot(v_ref[:, start:stop], low.astype(jnp.bfloat16), (1, 0))
        if start:
            high = jnp.exp(high - top)
            total += jnp.sum(high, 0, keepdims=True)
            mixed += dot(v_ref[:, :start], high.astype(jnp.bfloat16), (1, 0))
        out_ref[:, start:stop] = (mixed / total).astype(jnp.bfloat16)
        log_ref[0, :, start:stop] = top + jnp.log(total)


def backward_kernel(q_ref, k_ref, v_ref, g_ref, o_ref, log_ref, dq_ref, dk_ref, dv_ref):
    rows = q_ref.shape[1]

    @pl.when(lax.rem(pl.program_id(0), GROUP) == 0)
    def _():
        dk_ref[...] = jnp.zeros_like(dk_ref)
        dv_ref[...] = jnp.zeros_like(dv_ref)

    key_rows = k_ref[...].T
    value_rows = v_ref[...].T
    for start in range(0, rows, QB):
        stop = start + QB
        query = q_ref[:, start:stop]
        grad = g_ref[:, start:stop]
        log_sum = log_ref[0, :, start:stop]
        centre = jnp.sum(
            grad.astype(jnp.float32) * o_ref[:, start:stop].astype(jnp.float32), 0, keepdims=True
        )
        grad_query = None
        for first, last in ((start, stop), (0, start)):
            if first == last:
                continue
            scores = dot(key_rows[first:last], query, (1, 0))
            if first == start:
                scores = diagonal(scores)
            prob = jnp.exp(scores - log_sum)
            grad_prob = dot(value_rows[first:last], grad, (1, 0))
            grad_score = (prob * (grad_prob - centre)).astype(jnp.bfloat16)
            part = dot(k_ref[:, first:last], grad_score, (1, 0))
            grad_query = part if grad_query is None else grad_query + part
            dk_ref[:, first:last] += dot(query, grad_score, (1, 1))
            dv_ref[:, first:last] += dot(grad, prob.astype(jnp.bfloat16), (1, 1))
        dq_ref[:, start:stop] = grad_query * SCALE


def attend_forward(query, key, value):
    rows = query.shape[1]
    head = pl.BlockSpec((HEAD_DIM, rows), lambda j: (j, 0))
    shared = pl.BlockSpec((HEAD_DIM, rows), lambda j: (j // GROUP, 0))
    return pl.pallas_call(
        forward_kernel,
        grid=(HEADS,),
        in_specs=[head, shared, shared],
        out_specs=[head, pl.BlockSpec((1, 1, rows), lambda j: (j, 0, 0))],
        out_shape=[
            jax.ShapeDtypeStruct((D, rows), jnp.bfloat16),
            jax.ShapeDtypeStruct((HEADS, 1, rows), jnp.float32),
        ],
        compiler_params=pltpu.CompilerParams(vmem_limit_bytes=VMEM),
        cost_estimate=pl.CostEstimate(
            flops=4 * HEADS * rows * rows * HEAD_DIM,
            bytes_accessed=8 * D * rows,
            transcendentals=HEADS * rows * rows // 2,
        ),
        name="attend_forward",
    )(query, key, value)


def attend_backward(query, key, value, grad, attn, log_sums):
    rows = query.shape[1]
    head = pl.BlockSpec((HEAD_DIM, rows), lambda j: (j, 0))
    shared = pl.BlockSpec((HEAD_DIM, rows), lambda j: (j // GROUP, 0))
    return pl.pallas_call(
        backward_kernel,
        grid=(HEADS,),
        in_specs=[
            head, shared, shared, head, head, pl.BlockSpec((1, 1, rows), lambda j: (j, 0, 0))
        ],
        out_specs=[head, shared, shared],
        out_shape=[
            jax.ShapeDtypeStruct((D, rows), jnp.float32),
            jax.ShapeDtypeStruct((KV, rows), jnp.float32),
            jax.ShapeDtypeStruct((KV, rows), jnp.float32),
        ],
        compiler_params=pltpu.CompilerParams(vmem_limit_bytes=VMEM),
        cost_estimate=pl.CostEstimate(
            flops=10 * HEADS * rows * rows * HEAD_DIM,
            bytes_accessed=16 * D * rows,
            transcendentals=HEADS * rows * rows // 2,
        ),
        name="attend_backward",
    )(query, key, value, grad, attn, log_sums)


def rope_tables(row_count):
    half = HEAD_DIM // 2
    position = jnp.arange(row_count, dtype=jnp.float32)
    frequency = THETA ** (-jnp.arange(half, dtype=jnp.float32) * 2.0 / HEAD_DIM)
    angle = frequency[:, None] * position[None, :]
    return (jnp.cos(angle), jnp.sin(angle))


def rotate(tensor, cosine, sine, direction):
    half = HEAD_DIM // 2
    rows = tensor.shape[1]
    split = tensor.reshape(-1, 2, half, rows)
    first_half, second_half = split[:, 0], split[:, 1]
    return jnp.stack(
        [
            first_half * cosine - direction * second_half * sine,
            second_half * cosine + direction * first_half * sine,
        ],
        1,
    ).reshape(tensor.shape)


def rms_norm(inputs, gain):
    scale_row = lax.rsqrt(jnp.mean(inputs * inputs, -1, keepdims=True) + EPS)
    normed = inputs * scale_row
    return (normed, scale_row, (normed * gain).astype(jnp.bfloat16))


def rms_back(grad_rows, normed, scale_row, gain):
    gain_grad = jnp.sum(grad_rows * normed, 0)
    weighted = grad_rows * gain
    return (
        gain_grad,
        scale_row * (weighted - normed * jnp.mean(weighted * normed, -1, keepdims=True)),
    )


def gather(weight):
    return lax.all_gather(weight, "shard", axis=0, tiled=True)


def scatter(grad):
    return lax.psum_scatter(grad, "shard", scatter_dimension=0, tiled=True)


def widen(totals):
    return [total.astype(jnp.float32) for total in totals]


def shards(
    tokens, lengths, cotangent, w_query, w_key, w_value, w_out, w_gate, w_up, w_down,
    gain_attn, gain_ffn,
):
    row_count = tokens.shape[0]
    low_type = jnp.bfloat16
    live_mask = (lax.iota(jnp.int32, row_count) < lengths[0]).astype(jnp.float32)[:, None]
    first = gather(
        jnp.concatenate([w_query, w_key, w_value, gain_attn[:, None], gain_ffn[:, None]], 1)
    )
    width = D + 2 * KV
    qkv_full = first[:, :width]
    gain_one = first[:, width].astype(jnp.float32)
    gain_two = first[:, width + 1].astype(jnp.float32)
    out_full = gather(w_out)
    gate_full = gather(w_gate)
    up_full = gather(w_up)
    down_full = gather(w_down)

    inputs = tokens.astype(jnp.float32)
    normed_one, scale_one, hidden_one = rms_norm(inputs, gain_one)
    cosine, sine = rope_tables(row_count)
    qkv = dot(qkv_full, hidden_one, (0, 1))
    query_rot = (rotate(qkv[:D], cosine, sine, 1.0).astype(low_type) * SCALE).astype(low_type)
    key_rot = rotate(qkv[D : D + KV], cosine, sine, 1.0).astype(low_type)
    values = qkv[D + KV :].astype(low_type)
    attn, log_sums = attend_forward(query_rot, key_rot, values)
    mixed = inputs + dot(attn, out_full, (0, 0))
    normed_two, scale_two, hidden_two = rms_norm(mixed, gain_two)
    gate = dot(hidden_two, gate_full, (1, 0))
    up_proj = dot(hidden_two, up_full, (1, 0))
    sigmoid_gate = jax.nn.sigmoid(gate)
    activated = gate * sigmoid_gate
    product_low = (activated * up_proj).astype(low_type)

    grad_rows = cotangent.astype(jnp.float32) * live_mask
    grad_low = grad_rows.astype(low_type)
    grad_down = dot(product_low, grad_low, (0, 0)).astype(low_type)
    grad_product = dot(grad_low, down_full, (1, 1)).astype(low_type).astype(jnp.float32)
    silu_slope = sigmoid_gate * (1.0 + gate * (1.0 - sigmoid_gate))
    grad_gate_act = (grad_product * up_proj * silu_slope).astype(low_type)
    grad_up_act = (grad_product * activated).astype(low_type)
    grad_gate = dot(hidden_two, grad_gate_act, (0, 0)).astype(low_type)
    grad_up = dot(hidden_two, grad_up_act, (0, 0)).astype(low_type)
    grad_gate_act, grad_up_act, grad_down, grad_gate, grad_up = lax.optimization_barrier(
        (grad_gate_act, grad_up_act, grad_down, grad_gate, grad_up)
    )
    early = lax.psum((scatter(grad_down), scatter(grad_gate), scatter(grad_up)), "rep")
    output = (mixed + dot(product_low, down_full, (1, 0))) * live_mask
    grad_hidden_two = dot(grad_gate_act, gate_full, (1, 1)) + dot(grad_up_act, up_full, (1, 1))
    grad_gain_two, grad_norm_two = rms_back(grad_hidden_two, normed_two, scale_two, gain_two)
    grad_mixed = grad_rows + grad_norm_two
    grad_branch = grad_mixed.astype(low_type)
    grad_out = dot(attn, grad_branch, (1, 0)).astype(low_type)
    grad_attn = dot(out_full, grad_branch, (1, 1)).astype(low_type)
    grad_query_rot, grad_key_rot, grad_val = attend_backward(
        query_rot, key_rot, values, grad_attn, attn, log_sums
    )
    grad_qkv = jnp.concatenate(
        [
            rotate(grad_query_rot, cosine, sine, -1.0).astype(low_type),
            rotate(grad_key_rot, cosine, sine, -1.0).astype(low_type),
            grad_val.astype(low_type),
        ],
        0,
    )
    grad_qkv_w = dot(hidden_one, grad_qkv, (0, 1))
    grad_hidden_one = dot(grad_qkv, qkv_full, (0, 1))
    grad_gain_one, grad_norm_one = rms_back(grad_hidden_one, normed_one, scale_one, gain_one)
    grad_inputs = grad_mixed + grad_norm_one
    last = jnp.concatenate(
        [grad_qkv_w, grad_gain_one[:, None], grad_gain_two[:, None]], 1
    )
    late = (scatter(grad_out), scatter(last.astype(low_type)))
    early, late = lax.optimization_barrier((early, late))
    total_down, total_gate, total_up = widen(early)
    total_out, total_last = widen(lax.psum(late, "rep"))
    return (
        output,
        grad_inputs,
        total_last[:, :D],
        total_last[:, D : D + KV],
        total_last[:, D + KV : width],
        total_out,
        total_gate,
        total_up,
        total_down,
        total_last[:, width],
        total_last[:, width + 1],
    )


def solution(mesh):
    placed = (
        P(("rep", "shard"), None),
        P(("rep", "shard")),
        P(("rep", "shard"), None),
        P("shard", None),
        P("shard", None),
        P("shard", None),
        P("shard", None),
        P("shard", None),
        P("shard", None),
        P("shard", None),
        P("shard"),
        P("shard"),
    )
    return jax.shard_map(
        shards,
        mesh=mesh,
        in_specs=placed,
        out_specs=(
            P(("rep", "shard"), None),
            P(("rep", "shard"), None),
            P("shard", None),
            P("shard", None),
            P("shard", None),
            P("shard", None),
            P("shard", None),
            P("shard", None),
            P("shard", None),
            P("shard"),
            P("shard"),
        ),
        check_vma=False,
    )
```
